32 devices in a mesh: layer: 2 (over y), rows: 16 (over z, x, core).
Axes of the slice: x: 2, y: 2, z: 4, core: 2. Of those that a mesh axis runs over, the one named last changes fastest.
Arguments:
- weights: bfloat16 [2, 3712, 8192], P('layer', 'rows'), may hold values from -150 to 150
- sketch: bfloat16 [8192, 128], P('rows'), may hold values from -6 to 6
Outputs:
- base: bfloat16 [3712, 8192], P('rows', 'layer')
- range_basis: float32 [2, 3712, 128], P('layer', 'rows')
- lora_left: float32 [2, 3712, 128], P('layer', 'rows')
- lora_right: float32 [2, 8192, 128], P('layer', 'rows')
The draws below stay inside these ranges and needn't reach their ends.
All inputs are finite; a program needn't handle non-finite values.
Results may differ from the reference program's by a relative error of at most 0.002.
The reference program's roundings to bfloat16 on the way count: a program that leaves them out, or rounds other values in their place, can miss the bound.
Values may be sent and summed in bfloat16 or wider, within the bound.
A program may use at most 64 MiB of HBM per device.

```python
import math
import jax
import jax.numpy as jnp
from jax import lax

D = 8192
K = 128
FF = 3712
LAYERS = 2


def draw_weights(key, part):
    key = jax.random.fold_in(key, 7)
    key_rows, key_cols, key_noise = jax.random.split(key, 3)
    row_scale = jnp.exp(jax.random.uniform(key_rows, (LAYERS, FF, 1), jnp.float32, jnp.log(0.5), jnp.log(2.0)))
    col_scale = jnp.exp(jax.random.uniform(key_cols, (LAYERS, 1, D), jnp.float32, jnp.log(0.5), jnp.log(2.0)))
    position = jnp.arange(FF, dtype=jnp.float32).reshape(1, FF, 1) / (FF - 1)
    rising = jnp.exp(jnp.log(6.0) * position)
    noise = jnp.clip(jax.random.normal(key_noise, (LAYERS, FF, D), jnp.float32), -6.0, 6.0)
    return (noise * row_scale * col_scale * rising).astype(jnp.bfloat16)


def steps_of(key, shape, cuts, least, largest):
    def one(dim, shards_of):
        heights = jax.random.uniform(jax.random.fold_in(jax.random.fold_in(key, 6), dim), (shards_of,), jnp.float32, least / len(cuts), largest / len(cuts))
        return jnp.repeat(jnp.exp(heights), shape[dim] // shards_of).reshape((-1,) + (1,) * (len(shape) - dim - 1))

    factor_of = one(*cuts[0])
    for cut in cuts[1:]:
        factor_of = factor_of * one(*cut)
    return factor_of


def centred(own_key, shape, width, bound, cuts=(), kind=jnp.bfloat16):
    gain = steps_of(own_key, shape, cuts, -0.22, 0.18) if cuts else 1.0
    drawn = jax.random.normal(own_key, shape, jnp.float32) * width * gain
    return jnp.minimum(jnp.maximum(drawn, -bound), bound).astype(kind)


def setup_inputs(seed: int = 0) -> dict:
    key_of = jax.random.split(jax.random.key(seed), 3)
    weights = draw_weights(jax.random.fold_in(key_of[2], 71), 0)
    sketch = centred(key_of[1], (D, K), 1.0, 6.0, ((0, 16),))
    return {"weights": weights, "sketch": sketch}


def full_dot(left_side, right_side):
    return jnp.dot(left_side.astype(jnp.float32), right_side.astype(jnp.float32), precision=lax.Precision.HIGHEST, preferred_element_type=jnp.float32)

def reference(weights, sketch):
    layer_sum = jnp.zeros(weights.shape[1:], jnp.float32)
    for layer_idx in range(LAYERS):
        layer_sum = layer_sum + weights[layer_idx].astype(jnp.float32)
    base = (layer_sum / LAYERS).astype(jnp.bfloat16)
    base_wide = base.astype(jnp.float32)
    sketch_wide = sketch.astype(jnp.float32)
    basis_list = []
    left_list = []
    right_list = []
    for layer_idx in range(LAYERS):
        residual = weights[layer_idx].astype(jnp.float32) - base_wide
        sampled = full_dot(residual, sketch_wide)
        lower_tri = jnp.linalg.cholesky(full_dot(sampled.T, sampled))
        range_basis = jax.scipy.linalg.solve_triangular(lower_tri, sampled.T, lower=True).T
        basis_list.append(range_basis)
        co_space = full_dot(residual.T, range_basis)
        lower_row = jnp.linalg.cholesky(full_dot(co_space.T, co_space))
        projected = full_dot(residual, co_space)
        left_list.append(jax.scipy.linalg.solve_triangular(lower_row, projected.T, lower=True).T)
        right_list.append(math.sqrt(D) * jax.scipy.linalg.solve_triangular(lower_row, co_space.T, lower=True).T)
    return (base, jnp.stack(basis_list), jnp.stack(left_list), jnp.stack(right_list))
```

```python
import functools
import math

import jax
import jax.numpy as jnp
from jax import lax
from jax.experimental import pallas as pl
from jax.experimental.pallas import tpu as pltpu
from jax.sharding import PartitionSpec as P

MESH = pl.DeviceIdType.MESH
F32 = jnp.float32
BF16 = jnp.bfloat16
NN = (((1,), (0,)), ((), ()))
NT = (((1,), (1,)), ((), ()))


def flip(value, mask):
    bit = 0
    out = value
    while (1 << bit) <= mask:
        if (mask >> bit) & 1:
            out = out + (1 << bit) * (1 - 2 * ((value // (1 << bit)) % 2))
        bit += 1
    return out


def exact(left, right, dims=NN):
    return lax.dot_general(
        left, right, dims, precision=lax.Precision.HIGHEST, preferred_element_type=F32
    )


def fast(left, right, dims=NN):
    return lax.dot_general(left, right, dims, preferred_element_type=F32)


def split(value):
    high = value.astype(BF16)
    return high, (value - high.astype(F32)).astype(BF16)


def inverse_factor(aug, gram):
    size = gram.shape[0]
    row_of = lax.broadcasted_iota(jnp.int32, (size, size), 0)
    col_of = lax.broadcasted_iota(jnp.int32, (size, size), 1)
    aug[:, :size] = gram
    aug[:, size:] = jnp.where(row_of == col_of, 1.0, 0.0).astype(F32)
    row_id = lax.broadcasted_iota(jnp.int32, (size, 1), 0)
    lane_id = lax.broadcasted_iota(jnp.int32, (1, size), 1)

    def step(k, carry):
        row = aug[pl.ds(k, 1), :]
        left = aug[:, :size]
        right = aug[:, size:]
        hot = lane_id == k
        pivot = jnp.sum(jnp.where(hot, row[:, :size], 0.0), axis=1, keepdims=True)
        scale = lax.rsqrt(pivot)
        scale = scale * (1.5 - 0.5 * (pivot * scale) * scale)
        column = jnp.sum(jnp.where(hot, left, 0.0), axis=1, keepdims=True)
        unit = row * scale
        factor = jnp.where(row_id > k, column * scale, 0.0)
        here = row_id == k
        aug[:, :size] = jnp.where(here, unit[:, :size], left - factor * unit[:, :size])
        aug[:, size:] = jnp.where(here, unit[:, size:], right - factor * unit[:, size:])
        return carry

    lax.fori_loop(0, size, step, 0)
    return aug[:, size:]


def kernel(
    layers, devices,
    w_ref, sketch_ref,
    base_ref, basis_ref, left_ref, right_ref,
    w_in, w_far, e_high, e_low, base_v, s_v,
    y_part, y_in, y_all, p_part, p_in,
    gram, gram_in, inv, w_sum, w_half, z_own, z_recv, z_all,
    h_sum, h_in, h_all, aug,
    local_sem, wy_send, wy_recv, wx_send, wx_recv, s_send, s_recv,
    y_send, y_recv, ya_send, ya_recv, p_send, p_recv,
    g_send, g_recv, l_send, l_recv, ws_send, ws_recv,
    h_send, h_recv, ha_send, ha_recv, za_send, za_recv, zf_send, zf_recv,
):
    h = lax.axis_index("layer")
    r = lax.axis_index("rows")
    n = w_ref.shape[1]
    width = w_ref.shape[2]
    block = width // (2 * layers)
    chunks = devices // (2 * layers)
    x = (r // 2) % 2
    quarter = 2 * h + x
    layer_bits = layers.bit_length() - 1
    row_bits = devices.bit_length() - 1
    bits = [0] + list(range(2, row_bits))
    steps = len(bits)
    pending = []

    def send(src, dst, ss, rs, to_h, to_r):
        copy = pltpu.make_async_remote_copy(
            src_ref=src, dst_ref=dst, send_sem=ss, recv_sem=rs,
            device_id=(to_h, to_r), device_id_type=MESH,
        )
        copy.start()
        pending.append(copy)
        return copy

    barrier = pltpu.get_barrier_semaphore()
    total = layers * devices
    me = h * devices + r

    @pl.loop(1, total)
    def _(i):
        other = lax.rem(me + i, total)
        pl.semaphore_signal(
            barrier, inc=1, device_id=(other // devices, other % devices), device_id_type=MESH
        )

    pl.semaphore_wait(barrier, total - 1)

    def columns(q):
        return pl.ds(pl.multiple_of(q * block, block), block)

    far = []
    near = []
    own_x = flip(r, 2)
    for d in range(1, layers):
        to = flip(h, d)
        far.append(send(w_ref.at[0, :, columns(2 * to + (1 - x))], w_far.at[h],
                        wy_send.at[0, d], wy_recv.at[0, d], to, r))
    for d in range(1, layers):
        to = flip(h, d)
        near.append(send(w_ref.at[0, :, columns(2 * to + x)], w_in.at[h, 0],
                         wy_send.at[1, d], wy_recv.at[1, d], to, r))
    side = [send(w_ref.at[0, :, columns(2 * h + (1 - x))], w_in.at[h, 1],
                 wx_send.at[0], wx_recv.at[0], h, own_x)]
    mine0 = pltpu.make_async_copy(w_ref.at[0, :, columns(quarter)], w_in.at[h, 0], local_sem.at[0])
    mine1 = pltpu.make_async_copy(
        w_ref.at[0, :, columns(2 * h + (1 - x))], w_far.at[h], local_sem.at[1]
    )
    mine0.start()
    mine1.start()

    s_quarter = r // chunks
    s_slot = r % chunks
    sends_s = (s_quarter // 2) == h

    def s_copy(m):
        to = (m // 2) * 4 + (s_quarter % 2) * 2 + m % 2
        return to, pltpu.make_async_remote_copy(
            src_ref=sketch_ref, dst_ref=s_v.at[s_slot], send_sem=s_send.at[m],
            recv_sem=s_recv.at[s_slot], device_id=(h, to), device_id_type=MESH,
        )

    @pl.when(sends_s)
    def _():
        @pl.loop(0, devices // 2)
        def _(m):
            to, copy = s_copy(m)

            @pl.when(to != r)
            def _():
                copy.start()

            @pl.when(to == r)
            def _():
                pltpu.make_async_copy(sketch_ref, s_v.at[s_slot], s_recv.at[s_slot]).start()

    pad = e_high.shape[2]
    if pad > n:
        low = n // 16 * 16
        zero = jnp.zeros((layers, 2, pad - low, block), BF16)
        e_high[:, :, low:, :] = zero
        e_low[:, :, low:, :] = zero

    mine1.wait()
    for d in range(1, layers):
        far[d - 1].wait_recv()
        from_layer = flip(h, d)
        side.append(send(w_far.at[from_layer], w_in.at[from_layer, 1],
                         wx_send.at[d], wx_recv.at[d], h, own_x))

    tile = 128

    @pl.loop(0, block // tile)
    def _(t):
        at = pl.ds(pl.multiple_of(t * tile, tile), tile)
        total_w = w_far[0, :, at].astype(F32)
        for layer in range(1, layers):
            total_w = total_w + w_far[layer, :, at].astype(F32)
        base_v[1, :, at] = (total_w / layers).astype(BF16)

    out1 = pltpu.make_async_copy(base_v.at[1], base_ref.at[:, columns(1 - x)], local_sem.at[2])
    out1.start()

    def residuals(b):
        @pl.loop(0, block // tile)
        def _(t):
            at = pl.ds(pl.multiple_of(t * tile, tile), tile)
            total_w = w_in[0, b, :, at].astype(F32)
            for layer in range(1, layers):
                total_w = total_w + w_in[layer, b, :, at].astype(F32)
            base = (total_w / layers).astype(BF16)
            if b == 0:
                base_v[0, :, at] = base
            base = base.astype(F32)
            for layer in range(layers):
                high, low = split(w_in[layer, b, :, at].astype(F32) - base)
                e_high[layer, b, :n, at] = high
                e_low[layer, b, :n, at] = low

    def sampled(b):
        sketch = s_v[...].reshape(block, s_v.shape[2])
        for layer in range(layers):
            y_part[layer, b] = fast(e_high[layer, b], sketch) + fast(e_low[layer, b], sketch)

    mine0.wait()
    for copy in near:
        copy.wait_recv()
    residuals(0)
    out0 = pltpu.make_async_copy(base_v.at[0], base_ref.at[:, columns(x)], local_sem.at[3])
    out0.start()
    for c in range(chunks):
        pltpu.make_async_copy(sketch_ref, s_v.at[c], s_recv.at[c]).wait()
    sampled(0)
    for copy in side:
        copy.wait_recv()
    residuals(1)
    sampled(1)

    def to_owner(part, slots, ss, rs):
        copies = []
        for d in range(1, 2 * layers):
            to = flip(h, d // 2)
            copies.append(send(part.at[to, d % 2], slots.at[d - 1], ss.at[d], rs.at[d],
                               to, flip(r, 2 * (d % 2))))
        result = part[h, 0]
        for d in range(1, 2 * layers):
            copies[d - 1].wait_recv()
            result = result + slots[d - 1]
        return result

    y_own = to_owner(y_part, y_in, y_send, y_recv)
    y_all[h, 0] = y_own
    copies = []
    for d in range(1, 2 * layers):
        copies.append(send(y_all.at[h, 0], y_all.at[h, d % 2], ya_send.at[d], ya_recv.at[d],
                           flip(h, d // 2), flip(r, 2 * (d % 2))))
    for copy in copies:
        copy.wait_recv()

    def turned(b, layer):
        return y_all[layer, b].T

    def butterfly(total_ref, slots, ss, rs, partners):
        for i, (to_h, to_r) in enumerate(partners):
            copy = send(total_ref.at[i], slots.at[i], ss.at[i], rs.at[i], to_h, to_r)
            copy.wait_recv()
            total_ref[i + 1] = total_ref[i] + slots[i]
        return total_ref[len(partners)]

    gram[0] = exact(turned(0, h), y_all[h, 0]) + exact(turned(1, h), y_all[h, 1])
    g_total = [None]

    piece = width // devices
    for layer in range(layers):
        both = None
        for b in range(2):
            high, low = split(turned(b, layer))
            term = (
                fast(high, e_high[layer, b]) + fast(low, e_high[layer, b])
                + fast(high, e_low[layer, b])
            )
            both = term if both is None else both + term
        for c in range(chunks):
            w_sum[layer * chunks + c] = both[:, c * piece:(c + 1) * piece]

    start = 0
    offset = 0
    length = layers * chunks
    scatter = []
    for s, bit in enumerate(bits):
        half = length // 2
        up = (r // (1 << bit)) % 2
        keep = start + half * up
        give = start + half * (1 - up)
        w_copy = send(w_sum.at[pl.ds(give, half)], w_half.at[pl.ds(offset, half)],
                      ws_send.at[s], ws_recv.at[s], h, flip(r, 1 << bit))
        g_copy = send(gram.at[s], gram_in.at[s], g_send.at[s], g_recv.at[s], h, flip(r, 1 << bit))
        g_copy.wait_recv()
        gram[s + 1] = gram[s] + gram_in[s]
        if s == steps - 1:
            inv[h] = inverse_factor(aug, gram[s + 1])
            l_copies = [
                send(inv.at[h], inv.at[h], l_send.at[d], l_recv.at[d], flip(h, d), r)
                for d in range(1, layers)
            ]
            basis_ref[0] = exact(y_all[h, 0], inv[h], NT)[:n]
        w_copy.wait_recv()

        for i in range(half):
            w_sum[keep + i] = w_sum[keep + i] + w_half[offset + i]
        start = keep
        offset += half
        length = half
    for copy in l_copies:
        copy.wait_recv()

    chunk = start
    layer = chunk // chunks
    z_value = exact(inv[layer], w_sum[chunk])
    z_own[...] = z_value
    z_all[chunk] = z_value.astype(BF16)
    h_sum[0] = exact(z_value, z_value, NT)

    target_h = layer
    target_r = quarter * chunks + chunk % chunks
    stays = (target_h * devices + target_r) == me
    z_move = pltpu.make_async_remote_copy(
        src_ref=z_own, dst_ref=z_recv, send_sem=zf_send.at[0], recv_sem=zf_recv.at[0],
        device_id=(target_h, target_r), device_id_type=MESH,
    )
    z_stay = pltpu.make_async_copy(z_own, z_recv, zf_recv.at[0])

    partners = [(h, flip(r, 2))]
    partners += [(h, flip(r, 1 << bit)) for bit in bits[layer_bits:]]
    partners += [(flip(h, 1 << i), r) for i in range(layer_bits)]
    gather_at = [start]
    length = 1
    last = None
    z_order = list(range(steps))[::-1]
    z_copies = [None] * steps
    z_start = start

    def gather_step(s, z_start, length):
        there = pl.ds(z_start, length)
        return send(z_all.at[there], z_all.at[there], za_send.at[s], za_recv.at[s],
                    h, flip(r, 1 << bits[s]))

    rounds = max(steps, len(partners))
    z_copy = None
    for i in range(rounds):
        h_copy = None
        if i < len(partners):
            h_copy = send(h_sum.at[i], h_in.at[i], h_send.at[i], h_recv.at[i], *partners[i])
        if i < steps:
            s = z_order[i]
            if z_copy is not None:
                z_copy.wait_recv()
                up = (r // (1 << bits[s + 1])) % 2
                z_start = z_start - length * up
                length = 2 * length
            z_copy = gather_step(s, z_start, length)
        if i == 1:
            @pl.when(jnp.logical_not(stays))
            def _():
                z_move.start()

            @pl.when(stays)
            def _():
                z_stay.start()
        if h_copy is not None:
            h_copy.wait_recv()
            h_sum[i + 1] = h_sum[i] + h_in[i]
    h_all[layer] = h_sum[len(partners)]
    h_copies = []
    for d in range(1, layers):
        mask = 0
        for t in range(layer_bits):
            mask |= ((d >> (layer_bits - 1 - t)) & 1) << bits[t]
        h_copies.append(send(h_all.at[layer], h_all.at[layer], ha_send.at[d], ha_recv.at[d],
                             h, flip(r, mask)))
    for copy in h_copies:
        copy.wait_recv()
    z_copy.wait_recv()

    for layer_id in range(layers):
        for b in range(2):
            result = None
            for c in range(chunks):
                at = pl.ds(c * piece, piece)
                z_bf = z_all[layer_id * chunks + c]
                term = fast(e_high[layer_id, b, :, at], z_bf, NT)
                term = term + fast(e_low[layer_id, b, :, at], z_bf, NT)
                result = term if result is None else result + term
            p_part[layer_id, b] = result
    p_copies = []
    for d in range(1, 2 * layers):
        to = flip(h, d // 2)
        p_copies.append(send(p_part.at[to, d % 2], p_in.at[d - 1], p_send.at[d], p_recv.at[d],
                             to, flip(r, 2 * (d % 2))))

    row_inv = inverse_factor(aug, h_all[h])
    z_stay.wait()
    right_ref[0] = math.sqrt(width) * exact(row_inv, z_recv[...]).T
    p_own = p_part[h, 0]
    for d in range(1, 2 * layers):
        p_copies[d - 1].wait_recv()
        p_own = p_own + p_in[d - 1]
    left_ref[0] = exact(p_own, row_inv, NT)[:n]

    for copy in pending:
        copy.wait_send()

    @pl.when(jnp.logical_not(stays))
    def _():
        z_move.wait_send()

    @pl.when(sends_s)
    def _():
        @pl.loop(0, devices // 2)
        def _(m):
            to, copy = s_copy(m)

            @pl.when(to != r)
            def _():
                copy.wait_send()

    out0.wait()
    out1.wait()


def shards(weights, sketch):
    _, n, width = weights.shape
    rank = sketch.shape[1]
    layers = lax.axis_size("layer")
    devices = lax.axis_size("rows")
    block = width // (2 * layers)
    chunks = devices // (2 * layers)
    piece = width // devices
    pad = -(-n // 16) * 16
    steps = devices.bit_length() - 2
    rounds = steps + 1
    group = 2 * layers
    dma = pltpu.SemaphoreType.DMA
    vmem = pltpu.VMEM
    small = (rank, rank)
    scratch = [
        vmem((layers, 2, n, block), BF16),
        vmem((layers, n, block), BF16),
        vmem((layers, 2, pad, block), BF16),
        vmem((layers, 2, pad, block), BF16),
        vmem((2, n, block), BF16),
        vmem((chunks, piece, rank), BF16),
        vmem((layers, 2, pad, rank), F32),
        vmem((group - 1, pad, rank), F32),
        vmem((layers, 2, pad, rank), F32),
        vmem((layers, 2, pad, rank), F32),
        vmem((group - 1, pad, rank), F32),
        vmem((steps + 1, *small), F32),
        vmem((steps, *small), F32),
        vmem((layers, *small), F32),
        vmem((layers * chunks, rank, piece), F32),
        vmem((layers * chunks, rank, piece), F32),
        vmem((rank, piece), F32),
        vmem((rank, piece), F32),
        vmem((layers * chunks, rank, piece), BF16),
        vmem((rounds + 1, *small), F32),
        vmem((rounds, *small), F32),
        vmem((layers, *small), F32),
        vmem((rank, 2 * rank), F32),
        dma((4,)),
        dma((2, layers)), dma((2, layers)), dma((layers,)), dma((layers,)),
        dma((devices // 2,)), dma((chunks,)),
        dma((group,)), dma((group,)), dma((group,)), dma((group,)), dma((group,)), dma((group,)),
        dma((steps,)), dma((steps,)), dma((layers,)), dma((layers,)), dma((steps,)), dma((steps,)),
        dma((rounds,)), dma((rounds,)), dma((layers,)), dma((layers,)),
        dma((steps,)), dma((steps,)), dma((1,)), dma((1,)),
    ]
    anywhere = pl.BlockSpec(memory_space=pl.ANY)
    on_chip = pl.BlockSpec(memory_space=pltpu.VMEM)
    return pl.pallas_call(
        functools.partial(kernel, layers, devices),
        out_shape=(
            jax.ShapeDtypeStruct((n, width // layers), BF16),
            jax.ShapeDtypeStruct((1, n, rank), F32),
            jax.ShapeDtypeStruct((1, n, rank), F32),
            jax.ShapeDtypeStruct((1, piece, rank), F32),
        ),
        in_specs=[anywhere, anywhere],
        out_specs=(anywhere, on_chip, on_chip, on_chip),
        scratch_shapes=scratch,
        compiler_params=pltpu.CompilerParams(
            collective_id=0, has_side_effects=True, vmem_limit_bytes=56 * 1024 * 1024
        ),
    )(weights, sketch)


def solution(mesh):
    return jax.shard_map(
        shards,
        mesh=mesh,
        in_specs=(P("layer", "rows", None), P("rows", None)),
        out_specs=(
            P("rows", "layer"),
            P("layer", "rows", None),
            P("layer", "rows", None),
            P("layer", "rows", None),
        ),
        check_vma=False,
    )
```

```python
import functools
import math

import jax
import jax.numpy as jnp
from jax import lax
from jax.experimental import pallas as pl
from jax.experimental.pallas import tpu as pltpu
from jax.sharding import PartitionSpec as P

MESH = pl.DeviceIdType.MESH
F32 = jnp.float32
BF16 = jnp.bfloat16
NN = (((1,), (0,)), ((), ()))
NT = (((1,), (1,)), ((), ()))
PIECES = 4


def flip(value, mask):
    bit = 0
    out = value
    while (1 << bit) <= mask:
        if (mask >> bit) & 1:
            out = out + (1 << bit) * (1 - 2 * ((value // (1 << bit)) % 2))
        bit += 1
    return out


def exact(left, right, dims=NN):
    return lax.dot_general(
        left, right, dims, precision=lax.Precision.HIGHEST, preferred_element_type=F32
    )


def fast(left, right, dims=NN):
    return lax.dot_general(left, right, dims, preferred_element_type=F32)


def split(value):
    high = value.astype(BF16)
    return high, (value - high.astype(F32)).astype(BF16)


def begin_inverse(aug, gram):
    size = gram.shape[0]
    row_of = lax.broadcasted_iota(jnp.int32, (size, size), 0)
    col_of = lax.broadcasted_iota(jnp.int32, (size, size), 1)
    aug[:, :size] = gram
    aug[:, size:] = jnp.where(row_of == col_of, 1.0, 0.0).astype(F32)


def eliminate(aug, first, stop):
    size = aug.shape[0]
    row_id = lax.broadcasted_iota(jnp.int32, (size, 1), 0)
    lane_id = lax.broadcasted_iota(jnp.int32, (1, size), 1)

    def step(k, carry):
        row = aug[pl.ds(k, 1), :]
        left = aug[:, :size]
        right = aug[:, size:]
        hot = lane_id == k
        pivot = jnp.sum(jnp.where(hot, row[:, :size], 0.0), axis=1, keepdims=True)
        scale = lax.rsqrt(pivot)
        scale = scale * (1.5 - 0.5 * (pivot * scale) * scale)
        column = jnp.sum(jnp.where(hot, left, 0.0), axis=1, keepdims=True)
        unit = row * scale
        factor = jnp.where(row_id > k, column * scale, 0.0)
        here = row_id == k
        aug[:, :size] = jnp.where(here, unit[:, :size], left - factor * unit[:, :size])
        aug[:, size:] = jnp.where(here, unit[:, size:], right - factor * unit[:, size:])
        return carry

    lax.fori_loop(first, stop, step, 0)


def kernel(
    layers, devices,
    w_ref, sketch_ref,
    base_ref, basis_ref, left_ref, right_ref,
    w_in, w_far, e_high, e_low, base_v, s_v,
    y_part, y_in, y_all, p_part, p_in,
    gram, gram_in, inv, w_sum, w_half, z_own, z_recv, z_all,
    h_sum, h_in, h_all, aug,
    local_sem, wy_send, wy_recv, wx_send, wx_recv, s_send, s_recv,
    y_send, y_recv, ya_send, ya_recv, p_send, p_recv,
    g_send, g_recv, l_send, l_recv, ws_send, ws_recv,
    h_send, h_recv, ha_send, ha_recv, za_send, za_recv, zf_send, zf_recv,
):
    h = lax.axis_index("layer")
    r = lax.axis_index("rows")
    n = w_ref.shape[1]
    width = w_ref.shape[2]
    block = width // (2 * layers)
    chunks = devices // (2 * layers)
    x = (r // 2) % 2
    quarter = 2 * h + x
    layer_bits = layers.bit_length() - 1
    row_bits = devices.bit_length() - 1
    bits = [0] + list(range(2, row_bits))
    steps = len(bits)
    pending = []

    def send(src, dst, ss, rs, to_h, to_r):
        copy = pltpu.make_async_remote_copy(
            src_ref=src, dst_ref=dst, send_sem=ss, recv_sem=rs,
            device_id=(to_h, to_r), device_id_type=MESH,
        )
        copy.start()
        pending.append(copy)
        return copy

    barrier = pltpu.get_barrier_semaphore()
    total = layers * devices
    me = h * devices + r

    @pl.loop(1, total)
    def _(i):
        other = lax.rem(me + i, total)
        pl.semaphore_signal(
            barrier, inc=1, device_id=(other // devices, other % devices), device_id_type=MESH
        )

    pl.semaphore_wait(barrier, total - 1)

    def columns(q):
        return pl.ds(pl.multiple_of(q * block, block), block)

    own_x = flip(r, 2)
    part_width = block // PIECES

    def part(q, p):
        return pl.ds(pl.multiple_of(q * block + p * part_width, part_width), part_width)

    def within(p):
        return pl.ds(p * part_width, part_width)

    def over_layers(i):
        near, p = i // PIECES, i % PIECES
        copies = []
        for d in range(1, layers):
            to = flip(h, d)
            if near:
                copies.append(send(w_ref.at[0, :, part(2 * to + x, p)], w_in.at[h, 0, :, within(p)],
                                   wy_send.at[1, d, p], wy_recv.at[1, d, p], to, r))
            else:
                copies.append(send(w_ref.at[0, :, part(2 * to + (1 - x), p)],
                                   w_far.at[h, :, within(p)],
                                   wy_send.at[0, d, p], wy_recv.at[0, d, p], to, r))
        return copies

    def own_side(p):
        return [send(w_ref.at[0, :, part(2 * h + (1 - x), p)], w_in.at[h, 1, :, within(p)],
                     wx_send.at[0, p], wx_recv.at[0, p], h, own_x)]

    ahead = 2
    queue = [over_layers(i) for i in range(ahead)]
    side = [own_side(p) for p in range(ahead)]
    mine0 = pltpu.make_async_copy(w_ref.at[0, :, columns(quarter)], w_in.at[h, 0], local_sem.at[0])
    mine1 = pltpu.make_async_copy(
        w_ref.at[0, :, columns(2 * h + (1 - x))], w_far.at[h], local_sem.at[1]
    )
    mine0.start()
    mine1.start()

    s_quarter = r // chunks
    s_slot = r % chunks
    sends_s = (s_quarter // 2) == h

    def s_copy(m):
        to = (m // 2) * 4 + (s_quarter % 2) * 2 + m % 2
        return to, pltpu.make_async_remote_copy(
            src_ref=sketch_ref, dst_ref=s_v.at[s_slot], send_sem=s_send.at[m],
            recv_sem=s_recv.at[s_slot], device_id=(h, to), device_id_type=MESH,
        )

    @pl.when(sends_s)
    def _():
        @pl.loop(0, devices // 2)
        def _(m):
            to, copy = s_copy(m)

            @pl.when(to != r)
            def _():
                copy.start()

            @pl.when(to == r)
            def _():
                pltpu.make_async_copy(sketch_ref, s_v.at[s_slot], s_recv.at[s_slot]).start()

    pad = e_high.shape[2]
    if pad > n:
        low = n // 16 * 16
        zero = jnp.zeros((layers, 2, pad - low, block), BF16)
        e_high[:, :, low:, :] = zero
        e_low[:, :, low:, :] = zero

    tile = 128
    inner = part_width // tile

    def other_base(p):
        @pl.loop(p * inner, (p + 1) * inner)
        def _(t):
            at = pl.ds(pl.multiple_of(t * tile, tile), tile)
            total_w = w_far[0, :, at].astype(F32)
            for layer in range(1, layers):
                total_w = total_w + w_far[layer, :, at].astype(F32)
            base_v[1, :, at] = (total_w / layers).astype(BF16)

    def residuals(b, p):
        @pl.loop(p * inner, (p + 1) * inner)
        def _(t):
            at = pl.ds(pl.multiple_of(t * tile, tile), tile)
            total_w = w_in[0, b, :, at].astype(F32)
            for layer in range(1, layers):
                total_w = total_w + w_in[layer, b, :, at].astype(F32)
            base = (total_w / layers).astype(BF16)
            if b == 0:
                base_v[0, :, at] = base
            base = base.astype(F32)
            for layer in range(layers):
                high, low = split(w_in[layer, b, :, at].astype(F32) - base)
                e_high[layer, b, :n, at] = high
                e_low[layer, b, :n, at] = low

    def sampled(b, p):
        per = chunks // PIECES
        sketch = s_v[p * per:(p + 1) * per].reshape(part_width, s_v.shape[2])
        for layer in range(layers):
            term = fast(e_high[layer, b, :, within(p)], sketch)
            term = term + fast(e_low[layer, b, :, within(p)], sketch)
            if p == 0:
                y_part[layer, b] = term
            else:
                y_part[layer, b] = y_part[layer, b] + term

    mine1.wait()
    for i in range(2 * PIECES):
        near, p = i // PIECES, i % PIECES
        for copy in queue[i]:
            copy.wait_recv()
        if i + ahead < 2 * PIECES:
            queue.append(over_layers(i + ahead))
        if not near:
            for d in range(1, layers):
                source = flip(h, d)
                side[p].append(send(w_far.at[source, :, within(p)], w_in.at[source, 1, :, within(p)],
                                    wx_send.at[d, p], wx_recv.at[d, p], h, own_x))
            if p + ahead < PIECES:
                side.append(own_side(p + ahead))
            other_base(p)
            if p == PIECES - 1:
                out1 = pltpu.make_async_copy(
                    base_v.at[1], base_ref.at[:, columns(1 - x)], local_sem.at[2]
                )
                out1.start()
                mine0.wait()
                for c in range(chunks):
                    pltpu.make_async_copy(sketch_ref, s_v.at[c], s_recv.at[c]).wait()
        else:
            residuals(0, p)
            sampled(0, p)
            for copy in side[p]:
                copy.wait_recv()
            residuals(1, p)
            sampled(1, p)
    out0 = pltpu.make_async_copy(base_v.at[0], base_ref.at[:, columns(x)], local_sem.at[3])
    out0.start()

    def to_owner(part, slots, ss, rs):
        copies = []
        for d in range(1, 2 * layers):
            to = flip(h, d // 2)
            copies.append(send(part.at[to, d % 2], slots.at[d - 1], ss.at[d], rs.at[d],
                               to, flip(r, 2 * (d % 2))))
        result = part[h, 0]
        for d in range(1, 2 * layers):
            copies[d - 1].wait_recv()
            result = result + slots[d - 1]
        return result

    y_own = to_owner(y_part, y_in, y_send, y_recv)
    y_all[h, 0] = y_own
    copies = []
    for d in range(1, 2 * layers):
        copies.append(send(y_all.at[h, 0], y_all.at[h, d % 2], ya_send.at[d], ya_recv.at[d],
                           flip(h, d // 2), flip(r, 2 * (d % 2))))

    def butterfly(total_ref, slots, ss, rs, partners):
        for i, (to_h, to_r) in enumerate(partners):
            copy = send(total_ref.at[i], slots.at[i], ss.at[i], rs.at[i], to_h, to_r)
            yield
            copy.wait_recv()
            total_ref[i + 1] = total_ref[i] + slots[i]

    gram[0] = exact(y_own.T, y_own)
    gram_sum = butterfly(gram, gram_in, g_send, g_recv,
                         [(h, flip(r, 1 << bit)) for bit in range(row_bits)])
    next(gram_sum)
    piece = width // devices
    for d in range(2 * layers):
        if d > 0:
            copies[d - 1].wait_recv()
        layer, b = flip(h, d // 2), d % 2
        high, low = split(y_all[layer, b].T)
        for c in range(chunks):
            at = pl.ds(c * piece, piece)
            e_part = e_high[layer, b, :, at]
            term = fast(high, e_part) + fast(low, e_part) + fast(high, e_low[layer, b, :, at])
            if b == 0:
                w_sum[layer * chunks + c] = term
            else:
                w_sum[layer * chunks + c] = w_sum[layer * chunks + c] + term
        if d < 2 * layers - 1:
            next(gram_sum, None)

    rank = gram.shape[1]
    start = 0
    offset = 0
    length = layers * chunks
    done = 0
    for s, bit in enumerate(bits):
        half = length // 2
        up = (r // (1 << bit)) % 2
        keep = start + half * up
        give = start + half * (1 - up)
        w_copy = send(w_sum.at[pl.ds(give, half)], w_half.at[pl.ds(offset, half)],
                      ws_send.at[s], ws_recv.at[s], h, flip(r, 1 << bit))
        if s == 0:
            for _ in gram_sum:
                pass
            begin_inverse(aug, gram[row_bits])
        stop = rank // 6 + (rank - rank // 6) * s // (steps - 1)
        eliminate(aug, done, stop)
        done = stop
        if s == steps - 1:
            inv[h] = aug[:, rank:]
            l_copies = [
                send(inv.at[h], inv.at[h], l_send.at[d], l_recv.at[d], flip(h, d), r)
                for d in range(1, layers)
            ]
            basis_ref[0] = exact(y_all[h, 0], inv[h], NT)[:n]
        w_copy.wait_recv()
        for i in range(half):
            w_sum[keep + i] = w_sum[keep + i] + w_half[offset + i]
        start = keep
        offset += half
        length = half
    for copy in l_copies:
        copy.wait_recv()

    chunk = start
    layer = chunk // chunks
    z_value = exact(inv[layer], w_sum[chunk])
    z_own[...] = z_value
    z_all[chunk] = z_value.astype(BF16)
    h_sum[0] = exact(z_value, z_value, NT)

    target_h = layer
    target_r = quarter * chunks + chunk % chunks
    stays = (target_h * devices + target_r) == me
    z_move = pltpu.make_async_remote_copy(
        src_ref=z_own, dst_ref=z_recv, send_sem=zf_send.at[0], recv_sem=zf_recv.at[0],
        device_id=(target_h, target_r), device_id_type=MESH,
    )
    z_stay = pltpu.make_async_copy(z_own, z_recv, zf_recv.at[0])

    partners = [(h, flip(r, 2))]
    partners += [(flip(h, 1 << i), r) for i in range(layer_bits)]
    partners += [(h, flip(r, 1 << bit)) for bit in bits[layer_bits:]]
    h_part = butterfly(h_sum, h_in, h_send, h_recv, partners)

    def gather(z_start):
        length = 1
        for s in reversed(range(steps)):
            there = pl.ds(z_start, length)
            copy = send(z_all.at[there], z_all.at[there], za_send.at[s], za_recv.at[s],
                        h, flip(r, 1 << bits[s]))
            yield
            copy.wait_recv()
            z_start = z_start - length * ((r // (1 << bits[s])) % 2)
            length = 2 * length

    z_gather = gather(start)
    next(h_part)
    next(z_gather)
    for i in range(len(partners)):
        next(h_part, None)
        if i == len(partners) - 2:
            next(z_gather, None)
    h_all[layer] = h_sum[len(partners)]
    h_copies = []
    for d in range(1, layers):
        mask = 0
        for t in range(layer_bits):
            mask |= ((d >> (layer_bits - 1 - t)) & 1) << bits[t]
        h_copies.append(send(h_all.at[layer], h_all.at[layer], ha_send.at[d], ha_recv.at[d],
                             h, flip(r, mask)))

    @pl.when(jnp.logical_not(stays))
    def _():
        z_move.start()

    @pl.when(stays)
    def _():
        z_stay.start()

    for copy in h_copies:
        copy.wait_recv()
    begin_inverse(aug, h_all[h])
    eliminate(aug, 0, rank // 8)
    next(z_gather, None)
    eliminate(aug, rank // 8, rank // 4)
    for _ in z_gather:
        pass

    for layer_id in range(layers):
        for b in range(2):
            result = None
            for c in range(chunks):
                at = pl.ds(c * piece, piece)
                z_bf = z_all[layer_id * chunks + c]
                term = fast(e_high[layer_id, b, :, at], z_bf, NT)
                term = term + fast(e_low[layer_id, b, :, at], z_bf, NT)
                result = term if result is None else result + term
            p_part[layer_id, b] = result
    p_copies = []
    for d in range(1, 2 * layers):
        to = flip(h, d // 2)
        p_copies.append(send(p_part.at[to, d % 2], p_in.at[d - 1], p_send.at[d], p_recv.at[d],
                             to, flip(r, 2 * (d % 2))))

    eliminate(aug, rank // 4, rank)
    row_inv = aug[:, rank:]
    z_stay.wait()
    right_ref[0] = math.sqrt(width) * exact(row_inv, z_recv[...]).T
    p_own = p_part[h, 0]
    for d in range(1, 2 * layers):
        p_copies[d - 1].wait_recv()
        p_own = p_own + p_in[d - 1]
    left_ref[0] = exact(p_own, row_inv, NT)[:n]

    for copy in pending:
        copy.wait_send()

    @pl.when(jnp.logical_not(stays))
    def _():
        z_move.wait_send()

    @pl.when(sends_s)
    def _():
        @pl.loop(0, devices // 2)
        def _(m):
            to, copy = s_copy(m)

            @pl.when(to != r)
            def _():
                copy.wait_send()

    out0.wait()
    out1.wait()


def shards(weights, sketch):
    _, n, width = weights.shape
    rank = sketch.shape[1]
    layers = lax.axis_size("layer")
    devices = lax.axis_size("rows")
    block = width // (2 * layers)
    chunks = devices // (2 * layers)
    piece = width // devices
    pad = -(-n // 16) * 16
    steps = devices.bit_length() - 2
    rounds = steps + 1
    group = 2 * layers
    dma = pltpu.SemaphoreType.DMA
    vmem = pltpu.VMEM
    small = (rank, rank)
    scratch = [
        vmem((layers, 2, n, block), BF16),
        vmem((layers, n, block), BF16),
        vmem((layers, 2, pad, block), BF16),
        vmem((layers, 2, pad, block), BF16),
        vmem((2, n, block), BF16),
        vmem((chunks, piece, rank), BF16),
        vmem((layers, 2, pad, rank), F32),
        vmem((group - 1, pad, rank), F32),
        vmem((layers, 2, pad, rank), F32),
        vmem((layers, 2, pad, rank), F32),
        vmem((group - 1, pad, rank), F32),
        vmem((rounds + 1, *small), F32),
        vmem((rounds, *small), F32),
        vmem((layers, *small), F32),
        vmem((layers * chunks, rank, piece), F32),
        vmem((layers * chunks, rank, piece), F32),
        vmem((rank, piece), F32),
        vmem((rank, piece), F32),
        vmem((layers * chunks, rank, piece), BF16),
        vmem((rounds + 1, *small), F32),
        vmem((rounds, *small), F32),
        vmem((layers, *small), F32),
        vmem((rank, 2 * rank), F32),
        dma((4,)),
        dma((2, layers, PIECES)), dma((2, layers, PIECES)), dma((layers, PIECES)), dma((layers, PIECES)),
        dma((devices // 2,)), dma((chunks,)),
        dma((group,)), dma((group,)), dma((group,)), dma((group,)), dma((group,)), dma((group,)),
        dma((rounds,)), dma((rounds,)), dma((layers,)), dma((layers,)), dma((steps,)), dma((steps,)),
        dma((rounds,)), dma((rounds,)), dma((layers,)), dma((layers,)),
        dma((steps,)), dma((steps,)), dma((1,)), dma((1,)),
    ]
    anywhere = pl.BlockSpec(memory_space=pl.ANY)
    on_chip = pl.BlockSpec(memory_space=pltpu.VMEM)
    return pl.pallas_call(
        functools.partial(kernel, layers, devices),
        out_shape=(
            jax.ShapeDtypeStruct((n, width // layers), BF16),
            jax.ShapeDtypeStruct((1, n, rank), F32),
            jax.ShapeDtypeStruct((1, n, rank), F32),
            jax.ShapeDtypeStruct((1, piece, rank), F32),
        ),
        in_specs=[anywhere, anywhere],
        out_specs=(anywhere, on_chip, on_chip, on_chip),
        scratch_shapes=scratch,
        compiler_params=pltpu.CompilerParams(
            collective_id=0, has_side_effects=True, vmem_limit_bytes=56 * 1024 * 1024
        ),
    )(weights, sketch)


def solution(mesh):
    return jax.shard_map(
        shards,
        mesh=mesh,
        in_specs=(P("layer", "rows", None), P("rows", None)),
        out_specs=(
            P("rows", "layer"),
            P("layer", "rows", None),
            P("layer", "rows", None),
            P("layer", "rows", None),
        ),
        check_vma=False,
    )
```

```python
import functools
import math

import jax
import jax.numpy as jnp
from jax import lax
from jax.experimental import pallas as pl
from jax.experimental.pallas import tpu as pltpu
from jax.sharding import PartitionSpec as P

MESH = pl.DeviceIdType.MESH
F32 = jnp.float32
BF16 = jnp.bfloat16
NN = (((1,), (0,)), ((), ()))
NT = (((1,), (1,)), ((), ()))
PIECES = 4


def flip(value, mask):
    bit = 0
    out = value
    while (1 << bit) <= mask:
        if (mask >> bit) & 1:
            out = out + (1 << bit) * (1 - 2 * ((value // (1 << bit)) % 2))
        bit += 1
    return out


def exact(left, right, dims=NN):
    return lax.dot_general(
        left, right, dims, precision=lax.Precision.HIGHEST, preferred_element_type=F32
    )


def fast(left, right, dims=NN):
    return lax.dot_general(left, right, dims, preferred_element_type=F32)


def split(value):
    high = value.astype(BF16)
    return high, (value - high.astype(F32)).astype(BF16)


def begin_inverse(aug, gram):
    size = gram.shape[0]
    row_of = lax.broadcasted_iota(jnp.int32, (size, size), 0)
    col_of = lax.broadcasted_iota(jnp.int32, (size, size), 1)
    aug[:, :size] = gram
    aug[:, size:] = jnp.where(row_of == col_of, 1.0, 0.0).astype(F32)


def eliminate(aug, first, stop):
    size = aug.shape[0]
    row_id = lax.broadcasted_iota(jnp.int32, (size, 1), 0)
    lane_id = lax.broadcasted_iota(jnp.int32, (1, size), 1)

    def root(pivot):
        scale = lax.rsqrt(pivot)
        return scale * (1.5 - 0.5 * (pivot * scale) * scale)

    def pick(rows, hot):
        return jnp.sum(jnp.where(hot, rows, 0.0), axis=1, keepdims=True)

    def step(pair, carry):
        k = 2 * pair
        row_a = aug[pl.ds(k, 1), :]
        row_b = aug[pl.ds(k + 1, 1), :]
        left = aug[:, :size]
        right = aug[:, size:]
        hot_a = lane_id == k
        hot_b = lane_id == k + 1
        cross = pick(row_a[:, :size], hot_b)
        scale_a = root(pick(row_a[:, :size], hot_a))
        corner = pick(row_b[:, :size], hot_b)
        col_a = pick(left, hot_a)
        col_b = pick(left, hot_b)
        slope = cross * scale_a
        scale_b = root(corner - slope * slope)
        unit_a = row_a * scale_a
        unit_b = (row_b - slope * unit_a) * scale_b
        factor_a = col_a * scale_a
        factor_b = jnp.where(row_id > k + 1, (col_b - slope * factor_a) * scale_b, 0.0)
        factor_a = jnp.where(row_id > k + 1, factor_a, 0.0)
        for at, old in ((slice(0, size), left), (slice(size, 2 * size), right)):
            new = old - factor_a * unit_a[:, at] - factor_b * unit_b[:, at]
            new = jnp.where(row_id == k, unit_a[:, at], new)
            aug[:, at] = jnp.where(row_id == k + 1, unit_b[:, at], new)
        return carry

    lax.fori_loop(first // 2, stop // 2, step, 0)


def kernel(
    layers, devices,
    w_ref, sketch_ref,
    base_ref, basis_ref, left_ref, right_ref,
    w_in, w_far, e_high, e_low, base_v, s_v,
    y_part, y_in, y_all, p_part, p_in,
    gram, gram_in, inv, w_sum, w_half, z_own, z_recv, z_all,
    h_sum, h_in, h_all, aug,
    local_sem, wy_send, wy_recv, wx_send, wx_recv, s_send, s_recv,
    y_send, y_recv, ya_send, ya_recv, p_send, p_recv,
    g_send, g_recv, l_send, l_recv, ws_send, ws_recv,
    h_send, h_recv, ha_send, ha_recv, za_send, za_recv, zf_send, zf_recv,
):
    h = lax.axis_index("layer")
    r = lax.axis_index("rows")
    n = w_ref.shape[1]
    width = w_ref.shape[2]
    block = width // (2 * layers)
    chunks = devices // (2 * layers)
    x = (r // 2) % 2
    quarter = 2 * h + x
    layer_bits = layers.bit_length() - 1
    row_bits = devices.bit_length() - 1
    bits = [0] + list(range(2, row_bits))
    steps = len(bits)
    pending = []

    def send(src, dst, ss, rs, to_h, to_r):
        copy = pltpu.make_async_remote_copy(
            src_ref=src, dst_ref=dst, send_sem=ss, recv_sem=rs,
            device_id=(to_h, to_r), device_id_type=MESH,
        )
        copy.start()
        pending.append(copy)
        return copy

    barrier = pltpu.get_barrier_semaphore()
    me = h * devices + r

    def greet(to_h, to_r):
        pl.semaphore_signal(barrier, inc=1, device_id=(to_h, to_r), device_id_type=MESH)

    for d in range(1, 2 * layers):
        greet(flip(h, d // 2), flip(r, 2 * (d % 2)))

    @pl.loop(0, devices // 2)
    def _(m):
        to = (m // 2) * 4 + x * 2 + m % 2

        @pl.when(to != r)
        def _():
            greet(h, to)

    giver_quarter = r // chunks
    giver_chunk = h * chunks + r % chunks
    giver_h = giver_quarter // 2
    giver_r = 2 * (giver_quarter % 2)
    for s, bit in enumerate(bits):
        giver_r = giver_r + (1 << bit) * ((giver_chunk // (1 << (steps - 1 - s))) % 2)
    gets_own = giver_h * devices + giver_r == me

    @pl.when(jnp.logical_not(gets_own))
    def _():
        greet(giver_h, giver_r)
        pl.semaphore_wait(barrier, 2 * layers - 1 + devices // 2)

    @pl.when(gets_own)
    def _():
        pl.semaphore_wait(barrier, 2 * layers - 1 + devices // 2 - 1)

    def columns(q):
        return pl.ds(pl.multiple_of(q * block, block), block)

    own_x = flip(r, 2)
    part_width = block // PIECES

    def part(q, p):
        return pl.ds(pl.multiple_of(q * block + p * part_width, part_width), part_width)

    def within(p):
        return pl.ds(p * part_width, part_width)

    def over_layers(i):
        near, p = i // PIECES, i % PIECES
        copies = []
        for d in range(1, layers):
            to = flip(h, d)
            if near:
                copies.append(send(w_ref.at[0, :, part(2 * to + x, p)], w_in.at[h, 0, :, within(p)],
                                   wy_send.at[1, d, p], wy_recv.at[1, d, p], to, r))
            else:
                copies.append(send(w_ref.at[0, :, part(2 * to + (1 - x), p)],
                                   w_far.at[h, :, within(p)],
                                   wy_send.at[0, d, p], wy_recv.at[0, d, p], to, r))
        return copies

    def own_side(p):
        return [send(w_ref.at[0, :, part(2 * h + (1 - x), p)], w_in.at[h, 1, :, within(p)],
                     wx_send.at[0, p], wx_recv.at[0, p], h, own_x)]

    ahead = 2
    queue = [over_layers(i) for i in range(ahead)]
    side = [own_side(p) for p in range(ahead)]
    mine0 = pltpu.make_async_copy(w_ref.at[0, :, columns(quarter)], w_in.at[h, 0], local_sem.at[0])
    mine1 = pltpu.make_async_copy(
        w_ref.at[0, :, columns(2 * h + (1 - x))], w_far.at[h], local_sem.at[1]
    )
    mine0.start()
    mine1.start()

    s_quarter = r // chunks
    s_slot = r % chunks
    in_plane = (s_quarter // 2) == h
    is_root = jnp.logical_and(in_plane, (s_quarter % 2) == x)
    crosses = jnp.logical_and(in_plane, (s_quarter % 2) != x)
    other_slot = flip(r, 2) % chunks
    cross_copy = pltpu.make_async_remote_copy(
        src_ref=sketch_ref, dst_ref=s_v.at[s_slot], send_sem=s_send.at[0, 0],
        recv_sem=s_recv.at[s_slot], device_id=(h, own_x), device_id_type=MESH,
    )
    s_stay = pltpu.make_async_copy(sketch_ref, s_v.at[s_slot], s_recv.at[s_slot])

    def s_copy(m, which):
        to = (m // 2) * 4 + x * 2 + m % 2
        slot = other_slot if which else s_slot
        return to, pltpu.make_async_remote_copy(
            src_ref=s_v.at[slot] if which else sketch_ref, dst_ref=s_v.at[slot],
            send_sem=s_send.at[which, m],
            recv_sem=s_recv.at[slot], device_id=(h, to), device_id_type=MESH,
        )

    def spread(which, action):
        @pl.loop(0, devices // 2)
        def _(m):
            to, copy = s_copy(m, which)

            @pl.when(to != r)
            def _():
                action(copy)

    @pl.when(crosses)
    def _():
        cross_copy.start()

    @pl.when(is_root)
    def _():
        s_stay.start()
        spread(0, lambda copy: copy.start())

    pad = e_high.shape[2]
    if pad > n:
        low = n // 16 * 16
        zero = jnp.zeros((layers, 2, pad - low, block), BF16)
        e_high[:, :, low:, :] = zero
        e_low[:, :, low:, :] = zero

    tile = 128
    inner = part_width // tile

    def other_base(p):
        @pl.loop(p * inner, (p + 1) * inner)
        def _(t):
            at = pl.ds(pl.multiple_of(t * tile, tile), tile)
            total_w = w_far[0, :, at].astype(F32)
            for layer in range(1, layers):
                total_w = total_w + w_far[layer, :, at].astype(F32)
            base_v[1, :, at] = (total_w / layers).astype(BF16)

    def residuals(b, p):
        @pl.loop(p * inner, (p + 1) * inner)
        def _(t):
            at = pl.ds(pl.multiple_of(t * tile, tile), tile)
            total_w = w_in[0, b, :, at].astype(F32)
            for layer in range(1, layers):
                total_w = total_w + w_in[layer, b, :, at].astype(F32)
            base = (total_w / layers).astype(BF16)
            if b == 0:
                base_v[0, :, at] = base
            base = base.astype(F32)
            for layer in range(layers):
                high, low = split(w_in[layer, b, :, at].astype(F32) - base)
                e_high[layer, b, :n, at] = high
                e_low[layer, b, :n, at] = low

    def sampled(b, p):
        per = chunks // PIECES
        sketch = s_v[p * per:(p + 1) * per].reshape(part_width, s_v.shape[2])
        for layer in range(layers):
            term = fast(e_high[layer, b, :, within(p)], sketch)
            term = term + fast(e_low[layer, b, :, within(p)], sketch)
            if p == 0:
                y_part[layer, b] = term
            else:
                y_part[layer, b] = y_part[layer, b] + term

    @pl.when(is_root)
    def _():
        pltpu.make_async_copy(sketch_ref, s_v.at[other_slot], s_recv.at[other_slot]).wait()
        spread(1, lambda copy: copy.start())

    mine1.wait()
    for i in range(2 * PIECES):
        near, p = i // PIECES, i % PIECES
        for copy in queue[i]:
            copy.wait_recv()
        if i + ahead < 2 * PIECES:
            queue.append(over_layers(i + ahead))
        if not near:
            for d in range(1, layers):
                source = flip(h, d)
                side[p].append(send(w_far.at[source, :, within(p)], w_in.at[source, 1, :, within(p)],
                                    wx_send.at[d, p], wx_recv.at[d, p], h, own_x))
            if p + ahead < PIECES:
                side.append(own_side(p + ahead))
            other_base(p)
            if p == PIECES - 1:
                out1 = pltpu.make_async_copy(
                    base_v.at[1], base_ref.at[:, columns(1 - x)], local_sem.at[2]
                )
                out1.start()
                mine0.wait()
                for c in range(chunks):
                    @pl.when(jnp.logical_not(jnp.logical_and(is_root, other_slot == c)))
                    def _():
                        pltpu.make_async_copy(sketch_ref, s_v.at[c], s_recv.at[c]).wait()
        else:
            residuals(0, p)
            sampled(0, p)
            for copy in side[p]:
                copy.wait_recv()
            residuals(1, p)
            sampled(1, p)
    out0 = pltpu.make_async_copy(base_v.at[0], base_ref.at[:, columns(x)], local_sem.at[3])
    out0.start()

    def to_owner(part, slots, ss, rs):
        copies = []
        for d in range(1, 2 * layers):
            to = flip(h, d // 2)
            copies.append(send(part.at[to, d % 2], slots.at[d - 1], ss.at[d], rs.at[d],
                               to, flip(r, 2 * (d % 2))))
        result = part[h, 0]
        for d in range(1, 2 * layers):
            copies[d - 1].wait_recv()
            result = result + slots[d - 1]
        return result

    y_own = to_owner(y_part, y_in, y_send, y_recv)
    y_all[h, 0] = y_own
    copies = []
    for d in range(1, 2 * layers):
        copies.append(send(y_all.at[h, 0], y_all.at[h, d % 2], ya_send.at[d], ya_recv.at[d],
                           flip(h, d // 2), flip(r, 2 * (d % 2))))

    def butterfly(total_ref, slots, ss, rs, partners):
        for i, (to_h, to_r) in enumerate(partners):
            copy = send(total_ref.at[i], slots.at[i], ss.at[i], rs.at[i], to_h, to_r)
            yield
            copy.wait_recv()
            total_ref[i + 1] = total_ref[i] + slots[i]

    gram[0] = exact(y_own.T, y_own)
    gram_sum = butterfly(gram, gram_in, g_send, g_recv,
                         [(h, flip(r, 1 << bit)) for bit in range(row_bits)])
    next(gram_sum)
    piece = width // devices
    for d in range(2 * layers):
        if d > 0:
            copies[d - 1].wait_recv()
        layer, b = flip(h, d // 2), d % 2
        high, low = split(y_all[layer, b].T)
        for c in range(chunks):
            at = pl.ds(c * piece, piece)
            e_part = e_high[layer, b, :, at]
            term = fast(high, e_part) + fast(low, e_part) + fast(high, e_low[layer, b, :, at])
            if b == 0:
                w_sum[layer * chunks + c] = term
            else:
                w_sum[layer * chunks + c] = w_sum[layer * chunks + c] + term
        if d < 2 * layers - 1:
            next(gram_sum, None)

    rank = gram.shape[1]
    start = 0
    offset = 0
    length = layers * chunks
    done = 0
    for s, bit in enumerate(bits):
        half = length // 2
        up = (r // (1 << bit)) % 2
        keep = start + half * up
        give = start + half * (1 - up)
        w_copy = send(w_sum.at[pl.ds(give, half)], w_half.at[pl.ds(offset, half)],
                      ws_send.at[s], ws_recv.at[s], h, flip(r, 1 << bit))
        if s == 0:
            for _ in gram_sum:
                pass
            begin_inverse(aug, gram[row_bits])
        stop = (rank // 6 + (rank - rank // 6) * s // (steps - 1)) // 2 * 2
        eliminate(aug, done, stop)
        done = stop
        if s == steps - 1:
            inv[h] = aug[:, rank:]
            l_copies = [
                send(inv.at[h], inv.at[h], l_send.at[d], l_recv.at[d], flip(h, d), r)
                for d in range(1, layers)
            ]
            basis_ref[0] = exact(y_all[h, 0], inv[h], NT)[:n]
        w_copy.wait_recv()
        for i in range(half):
            w_sum[keep + i] = w_sum[keep + i] + w_half[offset + i]
        start = keep
        offset += half
        length = half
    for copy in l_copies:
        copy.wait_recv()

    chunk = start
    layer = chunk // chunks
    z_value = exact(inv[layer], w_sum[chunk])
    z_own[...] = z_value
    z_all[chunk] = z_value.astype(BF16)
    h_sum[0] = exact(z_value, z_value, NT)

    target_h = layer
    target_r = quarter * chunks + chunk % chunks
    stays = (target_h * devices + target_r) == me
    z_move = pltpu.make_async_remote_copy(
        src_ref=z_own, dst_ref=z_recv, send_sem=zf_send.at[0], recv_sem=zf_recv.at[0],
        device_id=(target_h, target_r), device_id_type=MESH,
    )
    z_stay = pltpu.make_async_copy(z_own, z_recv, zf_recv.at[0])

    partners = [(h, flip(r, 2))]
    partners += [(flip(h, 1 << i), r) for i in range(layer_bits)]
    partners += [(h, flip(r, 1 << bit)) for bit in bits[layer_bits:]]
    h_part = butterfly(h_sum, h_in, h_send, h_recv, partners)

    def gather(z_start):
        length = 1
        for s in reversed(range(steps)):
            there = pl.ds(z_start, length)
            copy = send(z_all.at[there], z_all.at[there], za_send.at[s], za_recv.at[s],
                        h, flip(r, 1 << bits[s]))
            yield
            copy.wait_recv()
            z_start = z_start - length * ((r // (1 << bits[s])) % 2)
            length = 2 * length

    z_gather = gather(start)
    next(h_part)
    next(z_gather)
    for i in range(len(partners)):
        next(h_part, None)
        if i == len(partners) - 2:
            next(z_gather, None)
    h_all[layer] = h_sum[len(partners)]
    h_copies = []
    for d in range(1, layers):
        mask = 0
        for t in range(layer_bits):
            mask |= ((d >> (layer_bits - 1 - t)) & 1) << bits[t]
        h_copies.append(send(h_all.at[layer], h_all.at[layer], ha_send.at[d], ha_recv.at[d],
                             h, flip(r, mask)))

    @pl.when(jnp.logical_not(stays))
    def _():
        z_move.start()

    @pl.when(stays)
    def _():
        z_stay.start()

    for copy in h_copies:
        copy.wait_recv()
    begin_inverse(aug, h_all[h])
    eliminate(aug, 0, rank // 8)
    next(z_gather, None)
    eliminate(aug, rank // 8, rank // 4)
    for _ in z_gather:
        pass

    for layer_id in range(layers):
        for b in range(2):
            result = None
            for c in range(chunks):
                at = pl.ds(c * piece, piece)
                z_bf = z_all[layer_id * chunks + c]
                term = fast(e_high[layer_id, b, :, at], z_bf, NT)
                term = term + fast(e_low[layer_id, b, :, at], z_bf, NT)
                result = term if result is None else result + term
            p_part[layer_id, b] = result
    p_copies = []
    for d in range(1, 2 * layers):
        to = flip(h, d // 2)
        p_copies.append(send(p_part.at[to, d % 2], p_in.at[d - 1], p_send.at[d], p_recv.at[d],
                             to, flip(r, 2 * (d % 2))))

    eliminate(aug, rank // 4, rank)
    row_inv = aug[:, rank:]
    z_stay.wait()
    right_ref[0] = math.sqrt(width) * exact(row_inv, z_recv[...]).T
    p_own = p_part[h, 0]
    for d in range(1, 2 * layers):
        p_copies[d - 1].wait_recv()
        p_own = p_own + p_in[d - 1]
    left_ref[0] = exact(p_own, row_inv, NT)[:n]

    for copy in pending:
        copy.wait_send()

    @pl.when(jnp.logical_not(stays))
    def _():
        z_move.wait_send()

    @pl.when(crosses)
    def _():
        cross_copy.wait_send()

    @pl.when(is_root)
    def _():
        spread(0, lambda copy: copy.wait_send())
        spread(1, lambda copy: copy.wait_send())

    out0.wait()
    out1.wait()


def shards(weights, sketch):
    _, n, width = weights.shape
    rank = sketch.shape[1]
    layers = lax.axis_size("layer")
    devices = lax.axis_size("rows")
    block = width // (2 * layers)
    chunks = devices // (2 * layers)
    piece = width // devices
    pad = -(-n // 16) * 16
    steps = devices.bit_length() - 2
    rounds = steps + 1
    group = 2 * layers
    dma = pltpu.SemaphoreType.DMA
    vmem = pltpu.VMEM
    small = (rank, rank)
    scratch = [
        vmem((layers, 2, n, block), BF16),
        vmem((layers, n, block), BF16),
        vmem((layers, 2, pad, block), BF16),
        vmem((layers, 2, pad, block), BF16),
        vmem((2, n, block), BF16),
        vmem((chunks, piece, rank), BF16),
        vmem((layers, 2, pad, rank), F32),
        vmem((group - 1, pad, rank), F32),
        vmem((layers, 2, pad, rank), F32),
        vmem((layers, 2, pad, rank), F32),
        vmem((group - 1, pad, rank), F32),
        vmem((rounds + 1, *small), F32),
        vmem((rounds, *small), F32),
        vmem((layers, *small), F32),
        vmem((layers * chunks, rank, piece), F32),
        vmem((layers * chunks, rank, piece), F32),
        vmem((rank, piece), F32),
        vmem((rank, piece), F32),
        vmem((layers * chunks, rank, piece), BF16),
        vmem((rounds + 1, *small), F32),
        vmem((rounds, *small), F32),
        vmem((layers, *small), F32),
        vmem((rank, 2 * rank), F32),
        dma((4,)),
        dma((2, layers, PIECES)), dma((2, layers, PIECES)), dma((layers, PIECES)), dma((layers, PIECES)),
        dma((2, devices // 2)), dma((chunks,)),
        dma((group,)), dma((group,)), dma((group,)), dma((group,)), dma((group,)), dma((group,)),
        dma((rounds,)), dma((rounds,)), dma((layers,)), dma((layers,)), dma((steps,)), dma((steps,)),
        dma((rounds,)), dma((rounds,)), dma((layers,)), dma((layers,)),
        dma((steps,)), dma((steps,)), dma((1,)), dma((1,)),
    ]
    anywhere = pl.BlockSpec(memory_space=pl.ANY)
    on_chip = pl.BlockSpec(memory_space=pltpu.VMEM)
    return pl.pallas_call(
        functools.partial(kernel, layers, devices),
        out_shape=(
            jax.ShapeDtypeStruct((n, width // layers), BF16),
            jax.ShapeDtypeStruct((1, n, rank), F32),
            jax.ShapeDtypeStruct((1, n, rank), F32),
            jax.ShapeDtypeStruct((1, piece, rank), F32),
        ),
        in_specs=[anywhere, anywhere],
        out_specs=(anywhere, on_chip, on_chip, on_chip),
        scratch_shapes=scratch,
        compiler_params=pltpu.CompilerParams(
            collective_id=0, has_side_effects=True, vmem_limit_bytes=56 * 1024 * 1024
        ),
    )(weights, sketch)


def solution(mesh):
    return jax.shard_map(
        shards,
        mesh=mesh,
        in_specs=(P("layer", "rows", None), P("rows", None)),
        out_specs=(
            P("rows", "layer"),
            P("layer", "rows", None),
            P("layer", "rows", None),
            P("layer", "rows", None),
        ),
        check_vma=False,
    )
```

```python
import functools
import math

import jax
import jax.numpy as jnp
from jax import lax
from jax.experimental import pallas as pl
from jax.experimental.pallas import tpu as pltpu
from jax.sharding import PartitionSpec as P

MESH = pl.DeviceIdType.MESH
F32 = jnp.float32
BF16 = jnp.bfloat16
NN = (((1,), (0,)), ((), ()))
NT = (((1,), (1,)), ((), ()))
PIECES = 4


def flip(value, mask):
    bit = 0
    out = value
    while (1 << bit) <= mask:
        if (mask >> bit) & 1:
            out = out + (1 << bit) * (1 - 2 * ((value // (1 << bit)) % 2))
        bit += 1
    return out


def exact(left, right, dims=NN):
    return lax.dot_general(
        left, right, dims, precision=lax.Precision.HIGHEST, preferred_element_type=F32
    )


def fast(left, right, dims=NN):
    return lax.dot_general(left, right, dims, preferred_element_type=F32)


def split(value):
    high = value.astype(BF16)
    return high, (value - high.astype(F32)).astype(BF16)


def begin_inverse(aug, gram):
    size = gram.shape[0]
    row_of = lax.broadcasted_iota(jnp.int32, (size, size), 0)
    col_of = lax.broadcasted_iota(jnp.int32, (size, size), 1)
    aug[:, :size] = gram
    aug[:, size:] = jnp.where(row_of == col_of, 1.0, 0.0).astype(F32)


def eliminate(aug, first, stop):
    size = aug.shape[0]
    row_id = lax.broadcasted_iota(jnp.int32, (size, 1), 0)
    lane_id = lax.broadcasted_iota(jnp.int32, (1, size), 1)

    def root(pivot):
        scale = lax.rsqrt(pivot)
        return scale * (1.5 - 0.5 * (pivot * scale) * scale)

    def pick(rows, hot):
        return jnp.sum(jnp.where(hot, rows, 0.0), axis=1, keepdims=True)

    def step(pair, carry):
        k = 2 * pair
        row_a = aug[pl.ds(k, 1), :]
        row_b = aug[pl.ds(k + 1, 1), :]
        left = aug[:, :size]
        right = aug[:, size:]
        hot_a = lane_id == k
        hot_b = lane_id == k + 1
        cross = pick(row_a[:, :size], hot_b)
        scale_a = root(pick(row_a[:, :size], hot_a))
        corner = pick(row_b[:, :size], hot_b)
        col_a = pick(left, hot_a)
        col_b = pick(left, hot_b)
        slope = cross * scale_a
        scale_b = root(corner - slope * slope)
        unit_a = row_a * scale_a
        unit_b = (row_b - slope * unit_a) * scale_b
        factor_a = col_a * scale_a
        factor_b = jnp.where(row_id > k + 1, (col_b - slope * factor_a) * scale_b, 0.0)
        factor_a = jnp.where(row_id > k + 1, factor_a, 0.0)
        for at, old in ((slice(0, size), left), (slice(size, 2 * size), right)):
            new = old - factor_a * unit_a[:, at] - factor_b * unit_b[:, at]
            new = jnp.where(row_id == k, unit_a[:, at], new)
            aug[:, at] = jnp.where(row_id == k + 1, unit_b[:, at], new)
        return carry

    lax.fori_loop(first // 2, stop // 2, step, 0)


def kernel(
    layers, devices,
    w_ref, sketch_ref,
    base_ref, basis_ref, left_ref, right_ref,
    w_in, w_far, e_high, e_low, base_v, s_v,
    y_part, y_in, y_all, p_part, p_in,
    gram, gram_in, inv, w_sum, w_half, z_own, z_recv, z_all,
    h_sum, h_in, h_all, aug,
    local_sem, wy_send, wy_recv, wx_send, wx_recv, s_send, s_recv,
    y_send, y_recv, ya_send, ya_recv, p_send, p_recv,
    g_send, g_recv, l_send, l_recv, ws_send, ws_recv,
    h_send, h_recv, ha_send, ha_recv, za_send, za_recv, zf_send, zf_recv,
):
    h = lax.axis_index("layer")
    r = lax.axis_index("rows")
    n = w_ref.shape[1]
    width = w_ref.shape[2]
    block = width // (2 * layers)
    chunks = devices // (2 * layers)
    x = (r // 2) % 2
    quarter = 2 * h + x
    layer_bits = layers.bit_length() - 1
    row_bits = devices.bit_length() - 1
    bits = [0] + list(range(2, row_bits))
    steps = len(bits)
    pending = []

    def send(src, dst, ss, rs, to_h, to_r):
        copy = pltpu.make_async_remote_copy(
            src_ref=src, dst_ref=dst, send_sem=ss, recv_sem=rs,
            device_id=(to_h, to_r), device_id_type=MESH,
        )
        copy.start()
        pending.append(copy)
        return copy

    barrier = pltpu.get_barrier_semaphore()
    me = h * devices + r

    def greet(to_h, to_r):
        pl.semaphore_signal(barrier, inc=1, device_id=(to_h, to_r), device_id_type=MESH)

    for d in range(1, 2 * layers):
        greet(flip(h, d // 2), flip(r, 2 * (d % 2)))

    @pl.loop(0, devices // 2)
    def _(m):
        to = (m // 2) * 4 + x * 2 + m % 2

        @pl.when(to != r)
        def _():
            greet(h, to)

    giver_quarter = r // chunks
    giver_chunk = h * chunks + r % chunks
    giver_h = giver_quarter // 2
    giver_r = 2 * (giver_quarter % 2)
    for s, bit in enumerate(bits):
        giver_r = giver_r + (1 << bit) * ((giver_chunk // (1 << (steps - 1 - s))) % 2)
    gets_own = giver_h * devices + giver_r == me

    @pl.when(jnp.logical_not(gets_own))
    def _():
        greet(giver_h, giver_r)
        pl.semaphore_wait(barrier, 2 * layers - 1 + devices // 2)

    @pl.when(gets_own)
    def _():
        pl.semaphore_wait(barrier, 2 * layers - 1 + devices // 2 - 1)

    def columns(q):
        return pl.ds(pl.multiple_of(q * block, block), block)

    own_x = flip(r, 2)
    part_width = block // PIECES

    def part(q, p):
        return pl.ds(pl.multiple_of(q * block + p * part_width, part_width), part_width)

    def within(p):
        return pl.ds(p * part_width, part_width)

    def over_layers(i):
        near, p = i // PIECES, i % PIECES
        copies = []
        for d in range(1, layers):
            to = flip(h, d)
            if near:
                copies.append(send(w_ref.at[0, :, part(2 * to + x, p)], w_in.at[h, 0, :, within(p)],
                                   wy_send.at[1, d, p], wy_recv.at[1, d, p], to, r))
            else:
                copies.append(send(w_ref.at[0, :, part(2 * to + (1 - x), p)],
                                   w_far.at[h, :, within(p)],
                                   wy_send.at[0, d, p], wy_recv.at[0, d, p], to, r))
        return copies

    def own_side(p):
        return [send(w_ref.at[0, :, part(2 * h + (1 - x), p)], w_in.at[h, 1, :, within(p)],
                     wx_send.at[0, p], wx_recv.at[0, p], h, own_x)]

    ahead = 2
    queue = [over_layers(i) for i in range(ahead)]
    side = [own_side(p) for p in range(ahead)]
    mine0 = pltpu.make_async_copy(w_ref.at[0, :, columns(quarter)], w_in.at[h, 0], local_sem.at[0])
    mine1 = pltpu.make_async_copy(
        w_ref.at[0, :, columns(2 * h + (1 - x))], w_far.at[h], local_sem.at[1]
    )
    mine0.start()
    mine1.start()

    s_quarter = r // chunks
    s_slot = r % chunks
    in_plane = (s_quarter // 2) == h
    is_root = jnp.logical_and(in_plane, (s_quarter % 2) == x)
    crosses = jnp.logical_and(in_plane, (s_quarter % 2) != x)
    other_slot = flip(r, 2) % chunks
    cross_copy = pltpu.make_async_remote_copy(
        src_ref=sketch_ref, dst_ref=s_v.at[s_slot], send_sem=s_send.at[0, 0],
        recv_sem=s_recv.at[s_slot], device_id=(h, own_x), device_id_type=MESH,
    )
    s_stay = pltpu.make_async_copy(sketch_ref, s_v.at[s_slot], s_recv.at[s_slot])

    def s_copy(m, which):
        to = (m // 2) * 4 + x * 2 + m % 2
        slot = other_slot if which else s_slot
        return to, pltpu.make_async_remote_copy(
            src_ref=s_v.at[slot] if which else sketch_ref, dst_ref=s_v.at[slot],
            send_sem=s_send.at[which, m],
            recv_sem=s_recv.at[slot], device_id=(h, to), device_id_type=MESH,
        )

    def spread(which, action):
        @pl.loop(0, devices // 2)
        def _(m):
            to, copy = s_copy(m, which)

            @pl.when(to != r)
            def _():
                action(copy)

    @pl.when(crosses)
    def _():
        cross_copy.start()

    @pl.when(is_root)
    def _():
        s_stay.start()
        spread(0, lambda copy: copy.start())

    pad = e_high.shape[2]
    if pad > n:
        low = n // 16 * 16
        zero = jnp.zeros((layers, 2, pad - low, block), BF16)
        e_high[:, :, low:, :] = zero
        e_low[:, :, low:, :] = zero

    tile = 128
    inner = part_width // tile

    def other_base(p):
        @pl.loop(p * inner, (p + 1) * inner)
        def _(t):
            at = pl.ds(pl.multiple_of(t * tile, tile), tile)
            total_w = w_far[0, :, at].astype(F32)
            for layer in range(1, layers):
                total_w = total_w + w_far[layer, :, at].astype(F32)
            base_v[1, :, at] = (total_w / layers).astype(BF16)

    def residuals(b, p):
        @pl.loop(p * inner, (p + 1) * inner)
        def _(t):
            at = pl.ds(pl.multiple_of(t * tile, tile), tile)
            total_w = w_in[0, b, :, at].astype(F32)
            for layer in range(1, layers):
                total_w = total_w + w_in[layer, b, :, at].astype(F32)
            base = (total_w / layers).astype(BF16)
            if b == 0:
                base_v[0, :, at] = base
            base = base.astype(F32)
            for layer in range(layers):
                high, low = split(w_in[layer, b, :, at].astype(F32) - base)
                e_high[layer, b, :n, at] = high
                e_low[layer, b, :n, at] = low

    def sampled(b, p):
        per = chunks // PIECES
        sketch = s_v[p * per:(p + 1) * per].reshape(part_width, s_v.shape[2])
        for layer in range(layers):
            term = fast(e_high[layer, b, :, within(p)], sketch)
            term = term + fast(e_low[layer, b, :, within(p)], sketch)
            if p == 0:
                y_part[layer, b] = term
            else:
                y_part[layer, b] = y_part[layer, b] + term

    @pl.when(is_root)
    def _():
        pltpu.make_async_copy(sketch_ref, s_v.at[other_slot], s_recv.at[other_slot]).wait()
        spread(1, lambda copy: copy.start())

    mine1.wait()
    for i in range(2 * PIECES):
        near, p = i // PIECES, i % PIECES
        for copy in queue[i]:
            copy.wait_recv()
        if i + ahead < 2 * PIECES:
            queue.append(over_layers(i + ahead))
        if not near:
            for d in range(1, layers):
                source = flip(h, d)
                side[p].append(send(w_far.at[source, :, within(p)], w_in.at[source, 1, :, within(p)],
                                    wx_send.at[d, p], wx_recv.at[d, p], h, own_x))
            if p + ahead < PIECES:
                side.append(own_side(p + ahead))
            other_base(p)
            if p == PIECES - 1:
                out1 = pltpu.make_async_copy(
                    base_v.at[1], base_ref.at[:, columns(1 - x)], local_sem.at[2]
                )
                out1.start()
                mine0.wait()
                for c in range(chunks):
                    @pl.when(jnp.logical_not(jnp.logical_and(is_root, other_slot == c)))
                    def _():
                        pltpu.make_async_copy(sketch_ref, s_v.at[c], s_recv.at[c]).wait()
        else:
            residuals(0, p)
            sampled(0, p)
            for copy in side[p]:
                copy.wait_recv()
            residuals(1, p)
            sampled(1, p)
    out0 = pltpu.make_async_copy(base_v.at[0], base_ref.at[:, columns(x)], local_sem.at[3])
    out0.start()

    def to_owner(part, slots, ss, rs):
        copies = []
        for d in range(1, 2 * layers):
            to = flip(h, d // 2)
            copies.append(send(part.at[to, d % 2], slots.at[d - 1], ss.at[d], rs.at[d],
                               to, flip(r, 2 * (d % 2))))
        result = part[h, 0]
        for d in range(1, 2 * layers):
            copies[d - 1].wait_recv()
            result = result + slots[d - 1]
        return result

    y_own = to_owner(y_part, y_in, y_send, y_recv)
    y_all[h, 0] = y_own
    copies = []
    for d in range(1, 2 * layers):
        copies.append(send(y_all.at[h, 0], y_all.at[h, d % 2], ya_send.at[d], ya_recv.at[d],
                           flip(h, d // 2), flip(r, 2 * (d % 2))))

    def butterfly(total_ref, slots, ss, rs, partners):
        for i, (to_h, to_r) in enumerate(partners):
            copy = send(total_ref.at[i], slots.at[i], ss.at[i], rs.at[i], to_h, to_r)
            yield
            copy.wait_recv()
            total_ref[i + 1] = total_ref[i] + slots[i]

    gram[0] = exact(y_own.T, y_own)
    gram_sum = butterfly(gram, gram_in, g_send, g_recv,
                         [(h, flip(r, 1 << bit)) for bit in range(row_bits)])
    next(gram_sum)
    rank = gram.shape[1]
    piece = width // devices
    for d in range(2 * layers):
        if d > 0:
            copies[d - 1].wait_recv()
        layer, b = flip(h, d // 2), d % 2
        high, low = split(y_all[layer, b].T)
        stacked = jnp.concatenate([high, low], axis=0)
        for c in range(chunks):
            at = pl.ds(c * piece, piece)
            e_part = e_high[layer, b, :, at]
            both = fast(stacked, e_part)
            term = both[:rank] + both[rank:] + fast(high, e_low[layer, b, :, at])
            if b == 0:
                w_sum[layer * chunks + c] = term
            else:
                w_sum[layer * chunks + c] = w_sum[layer * chunks + c] + term
        if d < 2 * layers - 1:
            next(gram_sum, None)

    start = 0
    offset = 0
    length = layers * chunks
    done = 0
    for s, bit in enumerate(bits):
        half = length // 2
        up = (r // (1 << bit)) % 2
        keep = start + half * up
        give = start + half * (1 - up)
        w_copy = send(w_sum.at[pl.ds(give, half)], w_half.at[pl.ds(offset, half)],
                      ws_send.at[s], ws_recv.at[s], h, flip(r, 1 << bit))
        if s == 0:
            for _ in gram_sum:
                pass
            begin_inverse(aug, gram[row_bits])
        stop = (rank // 6 + (rank - rank // 6) * s // (steps - 1)) // 2 * 2
        eliminate(aug, done, stop)
        done = stop
        if s == steps - 1:
            inv[h] = aug[:, rank:]
            l_copies = [
                send(inv.at[h], inv.at[h], l_send.at[d], l_recv.at[d], flip(h, d), r)
                for d in range(1, layers)
            ]
            basis_ref[0] = exact(y_all[h, 0], inv[h], NT)[:n]
        w_copy.wait_recv()
        for i in range(half):
            w_sum[keep + i] = w_sum[keep + i] + w_half[offset + i]
        start = keep
        offset += half
        length = half
    for copy in l_copies:
        copy.wait_recv()

    chunk = start
    layer = chunk // chunks
    z_value = exact(inv[layer], w_sum[chunk])
    z_own[...] = z_value
    z_all[chunk] = z_value.astype(BF16)
    h_sum[0] = exact(z_value, z_value, NT)

    target_h = layer
    target_r = quarter * chunks + chunk % chunks
    stays = (target_h * devices + target_r) == me
    z_move = pltpu.make_async_remote_copy(
        src_ref=z_own, dst_ref=z_recv, send_sem=zf_send.at[0], recv_sem=zf_recv.at[0],
        device_id=(target_h, target_r), device_id_type=MESH,
    )
    z_stay = pltpu.make_async_copy(z_own, z_recv, zf_recv.at[0])

    partners = [(h, flip(r, 2))]
    partners += [(flip(h, 1 << i), r) for i in range(layer_bits)]
    partners += [(h, flip(r, 1 << bit)) for bit in bits[layer_bits:]]
    h_part = butterfly(h_sum, h_in, h_send, h_recv, partners)

    def gather(z_start):
        length = 1
        for s in reversed(range(steps)):
            there = pl.ds(z_start, length)
            copy = send(z_all.at[there], z_all.at[there], za_send.at[s], za_recv.at[s],
                        h, flip(r, 1 << bits[s]))
            yield
            copy.wait_recv()
            z_start = z_start - length * ((r // (1 << bits[s])) % 2)
            length = 2 * length

    z_gather = gather(start)
    next(h_part)
    next(z_gather)
    for i in range(len(partners)):
        next(h_part, None)
        if i == len(partners) - 2:
            next(z_gather, None)
    h_all[layer] = h_sum[len(partners)]
    h_copies = []
    for d in range(1, layers):
        mask = 0
        for t in range(layer_bits):
            mask |= ((d >> (layer_bits - 1 - t)) & 1) << bits[t]
        h_copies.append(send(h_all.at[layer], h_all.at[layer], ha_send.at[d], ha_recv.at[d],
                             h, flip(r, mask)))

    @pl.when(jnp.logical_not(stays))
    def _():
        z_move.start()

    @pl.when(stays)
    def _():
        z_stay.start()

    for copy in h_copies:
        copy.wait_recv()
    begin_inverse(aug, h_all[h])
    eliminate(aug, 0, rank // 8)
    next(z_gather, None)
    eliminate(aug, rank // 8, rank // 4)
    for _ in z_gather:
        pass

    for layer_id in range(layers):
        result = None
        for c in range(chunks):
            at = pl.ds(c * piece, piece)
            z_bf = z_all[layer_id * chunks + c]
            term = fast(e_high[layer_id, :, :, at].reshape(2 * pad, piece), z_bf, NT)
            term = term + fast(e_low[layer_id, :, :, at].reshape(2 * pad, piece), z_bf, NT)
            result = term if result is None else result + term
        p_part[layer_id] = result.reshape(2, pad, rank)
    p_copies = []
    for d in range(1, 2 * layers):
        to = flip(h, d // 2)
        p_copies.append(send(p_part.at[to, d % 2], p_in.at[d - 1], p_send.at[d], p_recv.at[d],
                             to, flip(r, 2 * (d % 2))))

    eliminate(aug, rank // 4, rank)
    row_inv = aug[:, rank:]
    z_stay.wait()
    right_ref[0] = math.sqrt(width) * exact(row_inv, z_recv[...]).T
    p_own = p_part[h, 0]
    for d in range(1, 2 * layers):
        p_copies[d - 1].wait_recv()
        p_own = p_own + p_in[d - 1]
    left_ref[0] = exact(p_own, row_inv, NT)[:n]

    for copy in pending:
        copy.wait_send()

    @pl.when(jnp.logical_not(stays))
    def _():
        z_move.wait_send()

    @pl.when(crosses)
    def _():
        cross_copy.wait_send()

    @pl.when(is_root)
    def _():
        spread(0, lambda copy: copy.wait_send())
        spread(1, lambda copy: copy.wait_send())

    out0.wait()
    out1.wait()


def shards(weights, sketch):
    _, n, width = weights.shape
    rank = sketch.shape[1]
    layers = lax.axis_size("layer")
    devices = lax.axis_size("rows")
    block = width // (2 * layers)
    chunks = devices // (2 * layers)
    piece = width // devices
    pad = -(-n // 16) * 16
    steps = devices.bit_length() - 2
    rounds = steps + 1
    group = 2 * layers
    dma = pltpu.SemaphoreType.DMA
    vmem = pltpu.VMEM
    small = (rank, rank)
    scratch = [
        vmem((layers, 2, n, block), BF16),
        vmem((layers, n, block), BF16),
        vmem((layers, 2, pad, block), BF16),
        vmem((layers, 2, pad, block), BF16),
        vmem((2, n, block), BF16),
        vmem((chunks, piece, rank), BF16),
        vmem((layers, 2, pad, rank), F32),
        vmem((group - 1, pad, rank), F32),
        vmem((layers, 2, pad, rank), F32),
        vmem((layers, 2, pad, rank), F32),
        vmem((group - 1, pad, rank), F32),
        vmem((rounds + 1, *small), F32),
        vmem((rounds, *small), F32),
        vmem((layers, *small), F32),
        vmem((layers * chunks, rank, piece), F32),
        vmem((layers * chunks, rank, piece), F32),
        vmem((rank, piece), F32),
        vmem((rank, piece), F32),
        vmem((layers * chunks, rank, piece), BF16),
        vmem((rounds + 1, *small), F32),
        vmem((rounds, *small), F32),
        vmem((layers, *small), F32),
        vmem((rank, 2 * rank), F32),
        dma((4,)),
        dma((2, layers, PIECES)), dma((2, layers, PIECES)), dma((layers, PIECES)), dma((layers, PIECES)),
        dma((2, devices // 2)), dma((chunks,)),
        dma((group,)), dma((group,)), dma((group,)), dma((group,)), dma((group,)), dma((group,)),
        dma((rounds,)), dma((rounds,)), dma((layers,)), dma((layers,)), dma((steps,)), dma((steps,)),
        dma((rounds,)), dma((rounds,)), dma((layers,)), dma((layers,)),
        dma((steps,)), dma((steps,)), dma((1,)), dma((1,)),
    ]
    anywhere = pl.BlockSpec(memory_space=pl.ANY)
    on_chip = pl.BlockSpec(memory_space=pltpu.VMEM)
    return pl.pallas_call(
        functools.partial(kernel, layers, devices),
        out_shape=(
            jax.ShapeDtypeStruct((n, width // layers), BF16),
            jax.ShapeDtypeStruct((1, n, rank), F32),
            jax.ShapeDtypeStruct((1, n, rank), F32),
            jax.ShapeDtypeStruct((1, piece, rank), F32),
        ),
        in_specs=[anywhere, anywhere],
        out_specs=(anywhere, on_chip, on_chip, on_chip),
        scratch_shapes=scratch,
        compiler_params=pltpu.CompilerParams(
            collective_id=0, has_side_effects=True, vmem_limit_bytes=56 * 1024 * 1024
        ),
    )(weights, sketch)


def solution(mesh):
    return jax.shard_map(
        shards,
        mesh=mesh,
        in_specs=(P("layer", "rows", None), P("rows", None)),
        out_specs=(
            P("rows", "layer"),
            P("layer", "rows", None),
            P("layer", "rows", None),
            P("layer", "rows", None),
        ),
        check_vma=False,
    )
```
